256 devices in a mesh: depth: 8 (over z_hi, core), row: 8 (over z_lo, y), col: 4 (over x).
Axes of the slice: x: 4, y: 4, z: 8 (z_hi: 4, z_lo: 2; z = z_hi * 2 + z_lo), core: 2. Of those that a mesh axis runs over, the one named last changes fastest.
Arguments:
- inputs: bfloat16 [4096, 6144], P('depth', 'row'), may hold values from -6 to 6
- upstream: bfloat16 [4096, 6144], P('depth', 'row'), may hold values from -1.5 to 1.5
- w_in: bfloat16 [6144, 12288], P('row', 'col'), may hold values from -0.078125 to 0.078125
- w_out: bfloat16 [12288, 6144], P('col', 'row'), may hold values from -0.0546875 to 0.0546875
Outputs:
- grad_x: bfloat16 [4096, 6144], P(('depth', 'col'), 'row')
- grad_in: bfloat16 [6144, 12288], P('row', ('col', 'depth'))
- grad_out: bfloat16 [12288, 6144], P(('col', 'depth'), 'row')
The draws below stay inside these ranges and needn't reach their ends.
All inputs are finite; a program needn't handle non-finite values.
Results may differ from the reference program's by a relative error of at most 0.028.
Values may be sent and summed in bfloat16 or wider, within the bound.
No kernel may reach another device: no remote copies, remote signals or barrier semaphores. Data moves between devices by JAX's collectives and lax.ppermute only.
A program may use at most 128 MiB of HBM per device.

```python
import jax
import jax.numpy as jnp
from jax import lax

D = 6144
FF = 12288
TOKENS = 4096
N_DEPTH = 8
N_ROW = 8
N_COL = 4


def shard_levels(rng, dims, shards, smallest, largest):
    gain = 1.0
    for axis_at, shards_of in shards:
        steps = jax.random.uniform(jax.random.fold_in(jax.random.fold_in(rng, 6), axis_at), (shards_of,), jnp.float32, smallest / len(shards), largest / len(shards))
        gain = gain * jnp.repeat(jnp.exp(steps), dims[axis_at] // shards_of).reshape((-1,) + (1,) * (len(dims) - 1 - axis_at))
    return gain


def bell_draw(own_key, shape, scale, limit, shards=(), kind=jnp.bfloat16):
    array = jax.random.normal(own_key, shape, jnp.float32) * scale
    if len(shards) > 0:
        array = shard_levels(own_key, shape, shards, -0.22, 0.18) * array
    return jnp.clip(array, min=-limit, max=limit).astype(kind)


def setup_inputs(seed: int = 0) -> dict:
    key_list = jax.random.split(jax.random.key(seed), 5)
    return {
        "inputs": bell_draw(key_list[0], (TOKENS, D), 1.0, 6.0, ((0, 8), (1, 8))),
        "upstream": bell_draw(key_list[1], (TOKENS, D), 0.25, 1.5, ((0, 8), (1, 8))),
        "w_in": bell_draw(key_list[2], (D, FF), D ** -0.5, 0.078125, ((0, 8), (1, 4))),
        "w_out": bell_draw(key_list[3], (FF, D), FF ** -0.5, 0.0546875, ((0, 4), (1, 8))),
    }


def activation(values):
    return jax.nn.gelu(values, approximate=True)

def rounded(values):
    return lax.optimization_barrier(values.astype(jnp.bfloat16)).astype(jnp.float32)

def reference(inputs, upstream, w_in, w_out):
    width = D // N_ROW
    total_rows = inputs.shape[0]
    hidden = jnp.zeros((total_rows, FF), jnp.float32)
    d_act = jnp.zeros((total_rows, FF), jnp.float32)
    for block in range(N_ROW):
        lower = block * width
        hidden = hidden + rounded(jnp.dot(inputs[:, lower:lower + width], w_in[lower:lower + width], preferred_element_type=jnp.float32))
        d_act = d_act + rounded(jnp.dot(upstream[:, lower:lower + width], w_out[:, lower:lower + width].T, preferred_element_type=jnp.float32))
    act_full, pullback = jax.vjp(activation, hidden)
    act = act_full.astype(jnp.bfloat16)
    d_hidden = pullback(d_act)[0].astype(jnp.bfloat16)
    slab_rows = total_rows // N_DEPTH
    grad_in = jnp.zeros((D, FF), jnp.float32)
    grad_out = jnp.zeros((FF, D), jnp.float32)
    for slab_index in range(N_DEPTH):
        lower = slab_index * slab_rows
        grad_in = grad_in + rounded(jnp.dot(inputs[lower:lower + slab_rows].T, d_hidden[lower:lower + slab_rows], preferred_element_type=jnp.float32))
        grad_out = grad_out + rounded(jnp.dot(act[lower:lower + slab_rows].T, upstream[lower:lower + slab_rows], preferred_element_type=jnp.float32))
    columns = FF // N_COL
    grad_x = jnp.zeros((total_rows, D), jnp.float32)
    for block in range(N_COL):
        lower = block * columns
        grad_x = grad_x + rounded(jnp.dot(d_hidden[:, lower:lower + columns], w_in[:, lower:lower + columns].T, preferred_element_type=jnp.float32))
    return (grad_x.astype(jnp.bfloat16), grad_in.astype(jnp.bfloat16), grad_out.astype(jnp.bfloat16))
```

```python
import jax
import jax.numpy as jnp
from jax import lax
from jax.sharding import PartitionSpec as P

N_Z = 4
N_Y = 4
N_X = 4
SLAB = 512
WIDTH = 768
UNITS = 768
HALF = UNITS // 2
BF16 = jnp.bfloat16
F32 = jnp.float32

last_dims = (((1,), (1,)), ((), ()))
first_dims = (((0,), (0,)), ((), ()))


def activation(values):
    return jax.nn.gelu(values, approximate=True)


def activate(hidden, d_act):
    act_full, pullback = jax.vjp(activation, hidden)
    return act_full.astype(BF16), pullback(d_act)[0].astype(BF16)


def y_shift(values, by):
    perm = [(zl * N_Y + y, zl * N_Y + (y + by) % N_Y) for zl in range(2) for y in range(N_Y)]
    return lax.ppermute(values, "row", perm)


def zlo_swap(values):
    return lax.ppermute(values, "row", [(r, (r + N_Y) % 8) for r in range(8)])


def x_shift(values, by):
    return lax.ppermute(values, "col", [(c, (c + by) % N_X) for c in range(N_X)])


def zhi_shift(values, by):
    return lax.ppermute(values, "depth", [(d, (d + 2 * by) % 8) for d in range(8)])


def core_swap(values):
    return lax.ppermute(values, "depth", [(d, d ^ 1) for d in range(8)])


def row_order(rows, source):
    pick = source[:, None] == lax.broadcasted_iota(jnp.int32, (rows.shape[0],) * 2, 1)
    return jnp.dot(pick.astype(BF16), rows, preferred_element_type=F32).astype(BF16)


def ring_scatter(own, right, far, left, shift):
    far_up = shift(far[0], 1)
    far_down = shift(far[1], -1)
    up = jnp.stack([(right[0].astype(F32) + far_up.astype(F32)).astype(BF16), right[1]])
    down = jnp.stack([left[0], (left[1].astype(F32) + far_down.astype(F32)).astype(BF16)])
    up = shift(up, 1).astype(F32)
    down = shift(down, -1).astype(F32)
    return own[0].astype(F32) + up[0] + down[0], own[1].astype(F32) + up[1] + down[1]


def ring_gather(pair, shift):
    left = shift(pair, 1)
    right = shift(pair, -1)
    far0 = shift(left[0], 1)
    far1 = shift(right[1], -1)
    return [pair[0], right[0], far0, left[0]], [pair[1], right[1], far1, left[1]]


def on_device(inputs, upstream, w_in, w_out):
    depth = lax.axis_index("depth")
    row = lax.axis_index("row")
    x = lax.axis_index("col")
    zhi, core = depth // 2, depth % 2
    zlo, y = row // N_Y, row % N_Y

    own_at = zhi * UNITS + core * HALF
    other_at = zhi * UNITS + (1 - core) * HALF
    w_in = jnp.concatenate([lax.dynamic_slice_in_dim(w_in, at, HALF, 1) for at in (own_at, other_at)], 1)
    w_out = jnp.concatenate([lax.dynamic_slice_in_dim(w_out, at, HALF, 0) for at in (own_at, other_at)], 0)

    at = jnp.arange(SLAB, dtype=jnp.int32)
    yp, xp, zp, low = at // 128, at // 32 % 4, at // 16 % 2, at % 16
    source = (xp + x) % N_X * 128 + (yp + y) % N_Y * 32 + (zp + zlo) % 2 * 16 + low
    a_own = row_order(inputs, source)
    u_own = row_order(upstream, source)

    quarter = jnp.stack([v.reshape(4, 4, 32, WIDTH)[:, 0] for v in (a_own, u_own)])
    below = zhi_shift(quarter, 1)
    above = zhi_shift(quarter, -1)
    beyond = jnp.stack([zhi_shift(below[0], 1), zhi_shift(above[1], -1)])

    def spread(quarter):
        a_parts, u_parts = ring_gather(quarter, x_shift)
        return tuple(jnp.stack(parts, 1).reshape(SLAB, WIDTH) for parts in (a_parts, u_parts))

    def chunk(a, u):
        part_hidden = jnp.dot(a, w_in, preferred_element_type=F32).astype(BF16)
        part_grad = lax.dot_general(u, w_out, last_dims, preferred_element_type=F32).astype(BF16)
        pieces = [(part_hidden[128 * p:128 * p + 128], part_grad[128 * p:128 * p + 128]) for p in range(4)]
        hidden, d_act = ring_scatter(*pieces, y_shift)
        hidden, d_act = hidden.reshape(4, 2, 16, UNITS), d_act.reshape(4, 2, 16, UNITS)
        other = zlo_swap(jnp.stack([hidden[:, 1], d_act[:, 1]]).astype(BF16)).astype(F32)
        act, d_hidden = activate(hidden[:, 0] + other[0], d_act[:, 0] + other[1])
        pair = jnp.stack([act, d_hidden])
        pair = jnp.stack([pair, zlo_swap(pair)], 2).reshape(2, 128, UNITS)
        act, d_hidden = ring_gather(pair, y_shift)
        act, d_hidden = jnp.concatenate(act), jnp.concatenate(d_hidden)
        grad_in = lax.dot_general(a, d_hidden, first_dims, preferred_element_type=F32)
        grad_out = lax.dot_general(act, u, first_dims, preferred_element_type=F32)
        part_x = lax.dot_general(d_hidden, w_in, last_dims, preferred_element_type=F32).astype(BF16)
        part_x = part_x.reshape(4, 4, 32, WIDTH)
        pieces = [(part_x[:2, k], part_x[2:, k]) for k in range(4)]
        grad_x = jnp.concatenate(ring_scatter(*pieces, x_shift)).reshape(128, WIDTH)
        return grad_in, grad_out, grad_x

    grad_in, grad_out, grad_x = chunk(a_own, u_own)
    for quarter, by in ((above, 1), (below, -1), (beyond, 2)):
        more_in, more_out, part_x = chunk(*spread(quarter))
        grad_in, grad_out = grad_in + more_in, grad_out + more_out
        grad_x = grad_x + zhi_shift(part_x.astype(BF16), by).astype(F32)

    grad_in = grad_in[:, :HALF] + core_swap(grad_in[:, HALF:].astype(BF16)).astype(F32)
    grad_out = grad_out[:HALF] + core_swap(grad_out[HALF:].astype(BF16)).astype(F32)

    at = jnp.arange(128, dtype=jnp.int32)
    back = (at // 32 - y) % N_Y * 32 + (at // 16 - zlo) % 2 * 16 + at % 16
    grad_x = row_order(grad_x.astype(BF16), back)
    return (grad_x, grad_in.astype(BF16), grad_out.astype(BF16))


def solution(mesh):
    return jax.shard_map(
        on_device,
        mesh=mesh,
        in_specs=(P("depth", "row"), P("depth", "row"), P("row", "col"), P("col", "row")),
        out_specs=(
            P(("depth", "col"), "row"),
            P("row", ("col", "depth")),
            P(("col", "depth"), "row"),
        ),
        check_vma=False,
    )
```

```python
import jax
import jax.numpy as jnp
from jax import lax
from jax.sharding import PartitionSpec as P

RING = 4
ROWS = 128
WIDTH = 768
UNITS = 768
HALF = UNITS // 2
STREAMS = 3
STEP = HALF // STREAMS
BF16 = jnp.bfloat16
F32 = jnp.float32

last_dims = (((1,), (1,)), ((), ()))
first_dims = (((0,), (0,)), ((), ()))


def activation(values):
    return jax.nn.gelu(values, approximate=True)


def activate(hidden, d_act):
    act_full, pullback = jax.vjp(activation, hidden)
    return act_full.astype(BF16), pullback(d_act)[0].astype(BF16)


def y_shift(values, by):
    perm = [(zl * RING + y, zl * RING + (y + by) % RING) for zl in range(2) for y in range(RING)]
    return lax.ppermute(values, "row", perm)


def zlo_swap(values):
    return lax.ppermute(values, "row", [(r, (r + RING) % 8) for r in range(8)])


def x_shift(values, by):
    return lax.ppermute(values, "col", [(c, (c + by) % RING) for c in range(RING)])


def zhi_shift(values, by):
    return lax.ppermute(values, "depth", [(d, (d + 2 * by) % 8) for d in range(8)])


def core_swap(values):
    return lax.ppermute(values, "depth", [(d, d ^ 1) for d in range(8)])


def roll(pieces, by):
    return lax.dynamic_slice_in_dim(jnp.concatenate([pieces, pieces]), by, RING, 0)


def ring_scatter(own, right, far, left, shift):
    far_up = shift(far[0].astype(BF16), 1)
    far_down = shift(far[1].astype(BF16), -1)
    up = jnp.stack([(right[0].astype(F32) + far_up.astype(F32)).astype(BF16), right[1].astype(BF16)])
    down = jnp.stack([left[0].astype(BF16), (left[1].astype(F32) + far_down.astype(F32)).astype(BF16)])
    up = shift(up, 1).astype(F32)
    down = shift(down, -1).astype(F32)
    return own[0].astype(F32) + up[0] + down[0], own[1].astype(F32) + up[1] + down[1]


def ring_gather(pair, shift):
    left = shift(pair, 1)
    right = shift(pair, -1)
    far0 = shift(left[0], 1)
    far1 = shift(right[1], -1)
    return [pair[0], right[0], far0, left[0]], [pair[1], right[1], far1, left[1]]


def on_device(inputs, upstream, w_in, w_out):
    depth = lax.axis_index("depth")
    row = lax.axis_index("row")
    x = lax.axis_index("col")
    zhi, core = depth // 2, depth % 2
    y = row % RING

    own = jnp.stack([inputs, upstream])
    other = core_swap(own).reshape(2, RING, ROWS, WIDTH)
    own = own.reshape(2, RING, ROWS, WIDTH)
    plain = [jnp.stack([own[i], other[i]], 1) for i in range(2)]
    turned = [roll(v, y).reshape(-1, WIDTH) for v in plain]
    plain = [v.reshape(-1, WIDTH) for v in plain]

    def weights(stream, first):
        ats = [(first + k) % RING * UNITS + core * HALF + stream * STEP for k in range(RING)]
        return (
            jnp.concatenate([lax.dynamic_slice_in_dim(w_in, at, STEP, 1) for at in ats], 1),
            jnp.concatenate([lax.dynamic_slice_in_dim(w_out, at, STEP, 0) for at in ats], 0),
        )

    def forward(a, u, v_in, v_out):
        part_hidden = jnp.dot(a, v_in, preferred_element_type=F32).astype(BF16)
        part_grad = lax.dot_general(u, v_out, last_dims, preferred_element_type=F32).astype(BF16)
        return part_hidden, part_grad

    def backward(a, u, act, d_hidden, v_in):
        grad_in = lax.dot_general(d_hidden, a, first_dims, preferred_element_type=F32)
        grad_out = lax.dot_general(act, u, first_dims, preferred_element_type=F32)
        part_x = lax.dot_general(d_hidden, v_in, last_dims, preferred_element_type=F32)
        return grad_in, grad_out, part_x

    def first_half(a, u, stream):
        v_in, v_out = weights(stream, zhi)
        part_hidden, part_grad = forward(a, u, v_in, v_out)
        span = 2 * ROWS
        pieces = [(part_hidden[span * p:span * (p + 1)], part_grad[span * p:span * (p + 1)]) for p in range(RING)]
        return jnp.stack(ring_scatter(*pieces, y_shift)).astype(BF16), v_in

    def middle(pair):
        pair = pair.astype(F32) + zlo_swap(pair).astype(F32)
        act, d_hidden = ring_gather(jnp.stack(activate(pair[0], pair[1])), y_shift)
        return jnp.concatenate(act), jnp.concatenate(d_hidden)

    def last_half(a, u, act, d_hidden, v_in):
        grad_in, grad_out, part_x = backward(a, u, act, d_hidden, v_in)
        pieces = [(grad_in[STEP * k:STEP * (k + 1)], grad_out[STEP * k:STEP * (k + 1)]) for k in range(RING)]
        grad_in, grad_out = ring_scatter(*pieces, zhi_shift)
        return grad_in.astype(BF16), grad_out.astype(BF16), part_x

    off_in, off_out = weights(0, 0)
    parts = forward(*plain, off_in, off_out)
    parts, turned = lax.optimization_barrier((parts, turned))
    sums = lax.psum(parts, "row")

    one, v_one = first_half(*turned, 1)
    one, turned_late = lax.optimization_barrier((one, turned))
    two, v_two = first_half(*turned_late, 2)
    acts_one = middle(one)
    result_one = last_half(*turned, *acts_one, v_one)
    acts_two = middle(two)
    result_two = last_half(*turned, *acts_two, v_two)

    sums, _ = lax.optimization_barrier((sums, acts_two))
    acts = activate(sums[0].astype(F32), sums[1].astype(F32))
    grad_in, grad_out, off_x = backward(*plain, *acts, off_in)
    grads = [v.astype(BF16).reshape(RING, STEP, WIDTH) for v in (grad_in, grad_out)]
    grads = lax.psum_scatter(
        jnp.concatenate(grads, 1).reshape(-1, WIDTH),
        "depth",
        scatter_dimension=0,
        tiled=True,
        axis_index_groups=[[0, 2, 4, 6], [1, 3, 5, 7]],
    )

    grad_in = jnp.concatenate([v.T for v in (grads[:STEP], result_one[0], result_two[0])], 1)
    grad_out = jnp.concatenate([grads[STEP:], result_one[1], result_two[1]], 0)

    part_x = roll((result_one[2] + result_two[2]).reshape(RING, 2, ROWS, WIDTH), (-y) % RING)
    part_x = part_x + off_x.reshape(RING, 2, ROWS, WIDTH)
    part_x = part_x[:, 0] + core_swap(part_x[:, 1].astype(BF16)).astype(F32)
    part_x = roll(part_x.astype(BF16), x).reshape(RING, 2, ROWS // 2, WIDTH)
    grad_x = jnp.concatenate(ring_scatter(*part_x, x_shift))
    return (grad_x.astype(BF16), grad_in, grad_out)


def solution(mesh):
    return jax.shard_map(
        on_device,
        mesh=mesh,
        in_specs=(P("depth", "row"), P("depth", "row"), P("row", "col"), P("col", "row")),
        out_specs=(
            P(("depth", "col"), "row"),
            P("row", ("col", "depth")),
            P(("col", "depth"), "row"),
        ),
        check_vma=False,
    )
```

```python
import jax
import jax.numpy as jnp
from jax import lax
from jax.sharding import PartitionSpec as P

RING = 4
ROWS = 128
WIDTH = 768
UNITS = 768
HALF = UNITS // 2
STREAMS = 3
STEP = HALF // STREAMS
BF16 = jnp.bfloat16
F32 = jnp.float32

NEAR = (0, 3, 1, 2)
FAR = (0, 1, 3, 2)

last_dims = (((1,), (1,)), ((), ()))
first_dims = (((0,), (0,)), ((), ()))


def activation(values):
    return jax.nn.gelu(values, approximate=True)


def activate(hidden, d_act):
    act_full, pullback = jax.vjp(activation, hidden)
    return act_full.astype(BF16), pullback(d_act)[0].astype(BF16)


def y_swap(values, pair):
    return lax.ppermute(values, "row", [(r, r ^ pair) for r in range(8)])


def zlo_swap(values):
    return lax.ppermute(values, "row", [(r, r ^ 4) for r in range(8)])


def x_swap(values, pair):
    return lax.ppermute(values, "col", [(c, c ^ pair) for c in range(RING)])


def zhi_swap(values, pair):
    return lax.ppermute(values, "depth", [(d, d ^ (2 * pair)) for d in range(8)])


def core_swap(values):
    return lax.ppermute(values, "depth", [(d, d ^ 1) for d in range(8)])


def halve(kept, sent, swap, pairs):
    first = swap(sent.astype(BF16), pairs[0])
    both = kept.astype(F32) + first.astype(F32)
    span = both.shape[0] // 2
    return both[:span] + swap(both[span:].astype(BF16), pairs[1]).astype(F32), first


def double(own, swap, pairs):
    two = jnp.concatenate([own, swap(own, pairs[1])])
    return jnp.concatenate([two, swap(two, pairs[0])])


def on_device(inputs, upstream, w_in, w_out):
    depth = lax.axis_index("depth")
    x = lax.axis_index("col")
    zhi, core = depth // 2, depth % 2
    y = lax.axis_index("row") % RING

    def slabs(own, order):
        other = core_swap(own)
        ats = [(y ^ k) * ROWS for k in order]
        return jnp.concatenate([lax.dynamic_slice_in_dim(v, at, ROWS, 0) for at in ats for v in (own, other)])

    a = slabs(inputs, NEAR)
    u = slabs(upstream, FAR)

    def forward(stream, after):
        ats = [(zhi ^ k) * UNITS + core * HALF + stream * STEP for k in NEAR]
        v_in = jnp.concatenate([lax.dynamic_slice_in_dim(w_in, at, STEP, 1) for at in ats], 1)
        v_out = jnp.concatenate([lax.dynamic_slice_in_dim(w_out, at, STEP, 0) for at in ats], 0)
        part_hidden = jnp.dot(a, v_in, preferred_element_type=F32)
        part_grad = lax.dot_general(u, v_out, last_dims, preferred_element_type=F32)
        if after is not None:
            nothing = after[:1].astype(F32) * 0.0
            part_hidden, part_grad = part_hidden + nothing, part_grad + nothing
        part_hidden, part_grad = part_hidden.astype(BF16), part_grad.astype(BF16)
        span = part_hidden.shape[0] // 2
        hidden, came = halve(part_hidden[:span], part_hidden[span:], y_swap, (1, 3))
        d_act, _ = halve(part_grad[:span], part_grad[span:], y_swap, (3, 1))
        return hidden, d_act, v_in, came

    def backward(hidden, d_act, v_in):
        pair = jnp.stack([hidden, d_act]).astype(BF16)
        pair = pair.astype(F32) + zlo_swap(pair).astype(F32)
        act, d_hidden = activate(pair[0], pair[1])
        d_hidden = double(d_hidden, y_swap, (1, 3))
        act = double(act, y_swap, (3, 1))
        grad_in = lax.dot_general(d_hidden, a, first_dims, preferred_element_type=F32)
        grad_out = lax.dot_general(act, u, first_dims, preferred_element_type=F32)
        part_x = lax.dot_general(d_hidden, v_in, last_dims, preferred_element_type=F32)
        grad_in, _ = halve(grad_in[:2 * STEP], grad_in[2 * STEP:], zhi_swap, (1, 3))
        blocks = [grad_out[STEP * k:STEP * (k + 1)] for k in range(RING)]
        grad_out, _ = halve(
            jnp.concatenate([blocks[0], blocks[2]]), jnp.concatenate([blocks[1], blocks[3]]), zhi_swap, (3, 1)
        )
        return grad_in.astype(BF16).T, grad_out.astype(BF16), part_x

    results, came = [], None
    for stream in range(STREAMS):
        hidden, d_act, v_in, came = forward(stream, came)
        results.append(backward(hidden, d_act, v_in))
    grad_in = jnp.concatenate([r[0] for r in results], 1)
    grad_out = jnp.concatenate([r[1] for r in results], 0)

    part_x = sum(r[2] for r in results).reshape(RING, 2, ROWS, WIDTH)
    part_x = part_x[:, 0] + core_swap(part_x[:, 1].astype(BF16)).astype(F32)

    def rows_of(k):
        k = k ^ x ^ y
        at = jnp.where(k == 0, 0, jnp.where(k == 3, 1, k + 1))
        return lax.dynamic_index_in_dim(part_x, at, 0, keepdims=False)

    pieces = {k: rows_of(k) for k in range(RING)}
    cut = ROWS // 2
    upper = [pieces[k][:cut] for k in NEAR]
    lower = [pieces[k][cut:] for k in FAR]
    upper, _ = halve(jnp.concatenate(upper[:2]), jnp.concatenate(upper[2:]), x_swap, (1, 3))
    lower, _ = halve(jnp.concatenate(lower[:2]), jnp.concatenate(lower[2:]), x_swap, (3, 1))
    grad_x = jnp.concatenate([upper, lower]).astype(BF16)
    return (grad_x, grad_in, grad_out)


def solution(mesh):
    return jax.shard_map(
        on_device,
        mesh=mesh,
        in_specs=(P("depth", "row"), P("depth", "row"), P("row", "col"), P("col", "row")),
        out_specs=(
            P(("depth", "col"), "row"),
            P("row", ("col", "depth")),
            P(("col", "depth"), "row"),
        ),
        check_vma=False,
    )
```

```python
import jax
import jax.numpy as jnp
from jax import lax
from jax.sharding import PartitionSpec as P

RING = 4
SLAB = 512
ROWS = 128
LOW = 32
WIDTH = 768
UNITS = 768
HALF = UNITS // 2
BF16 = jnp.bfloat16
F32 = jnp.float32

NEAR = (0, 3, 1, 2)
FAR = (0, 1, 3, 2)

last_dims = (((1,), (1,)), ((), ()))
first_dims = (((0,), (0,)), ((), ()))


def activation(values):
    return jax.nn.gelu(values, approximate=True)


def activate(hidden, d_act):
    act_full, pullback = jax.vjp(activation, hidden)
    return act_full.astype(BF16), pullback(d_act)[0].astype(BF16)


def y_swap(values, pair):
    return lax.ppermute(values, "row", [(r, r ^ pair) for r in range(8)])


def zlo_swap(values):
    return lax.ppermute(values, "row", [(r, r ^ 4) for r in range(8)])


def x_swap(values, pair):
    return lax.ppermute(values, "col", [(c, c ^ pair) for c in range(RING)])


def zhi_swap(values, pair):
    return lax.ppermute(values, "depth", [(d, d ^ (2 * pair)) for d in range(8)])


def core_swap(values):
    return lax.ppermute(values, "depth", [(d, d ^ 1) for d in range(8)])


def halve(kept, sent, swap, pairs):
    both = kept.astype(F32) + swap(sent.astype(BF16), pairs[0]).astype(F32)
    span = both.shape[0] // 2
    return both[:span] + swap(both[span:].astype(BF16), pairs[1]).astype(F32)


def double(own, swap, pairs):
    two = jnp.concatenate([own, swap(own, pairs[1])])
    return jnp.concatenate([two, swap(two, pairs[0])])


def row_order(rows, source):
    pick = source[:, None] == lax.broadcasted_iota(jnp.int32, (source.shape[0], rows.shape[0]), 1)
    return jnp.dot(pick.astype(BF16), rows, preferred_element_type=F32).astype(BF16)


def on_device(inputs, upstream, w_in, w_out):
    depth = lax.axis_index("depth")
    x = lax.axis_index("col")
    zhi, core = depth // 2, depth % 2
    y = lax.axis_index("row") % RING

    ats = [zhi * UNITS + c * HALF for c in (core, 1 - core)]
    w_in = jnp.concatenate([lax.dynamic_slice_in_dim(w_in, at, HALF, 1) for at in ats], 1)
    w_out = jnp.concatenate([lax.dynamic_slice_in_dim(w_out, at, HALF, 0) for at in ats], 0)

    at = jnp.arange(SLAB, dtype=jnp.int32)

    def order(order_y, place):
        order_y, order_x = (jnp.array(o, jnp.int32) for o in (order_y, NEAR))
        return (order_x[place // LOW % RING] ^ x) * ROWS + (order_y[place // ROWS] ^ y) * LOW + place % LOW

    a_own = row_order(inputs, order(NEAR, at))
    u_own = row_order(upstream, order(FAR, at))

    quarter = jnp.stack([v.reshape(RING, RING, LOW, WIDTH)[:, 0] for v in (a_own, u_own)])
    got_1 = zhi_swap(quarter, 1)
    got_3 = zhi_swap(quarter, 3)
    got_2 = (zhi_swap(got_1[0], 3), zhi_swap(got_3[1], 1))

    def spread(quarter):
        one_a = x_swap(quarter[0], 1)
        three_u = x_swap(quarter[1], 3)
        far_a = x_swap(jnp.stack([quarter[0], one_a]), 3)
        far_u = x_swap(jnp.stack([quarter[1], three_u]), 1)
        a = jnp.stack([quarter[0], far_a[0], one_a, far_a[1]], 1)
        u = jnp.stack([quarter[1], three_u, far_u[0], far_u[1]], 1)
        return a.reshape(SLAB, WIDTH), u.reshape(SLAB, WIDTH)

    def chunk(a, u):
        part_hidden = jnp.dot(a, w_in, preferred_element_type=F32).astype(BF16)
        part_grad = lax.dot_general(u, w_out, last_dims, preferred_element_type=F32).astype(BF16)
        hidden = halve(part_hidden[:SLAB // 2], part_hidden[SLAB // 2:], y_swap, (1, 3))
        d_act = halve(part_grad[:SLAB // 2], part_grad[SLAB // 2:], y_swap, (3, 1))
        pair = jnp.stack([hidden, d_act]).astype(BF16)
        pair = pair.astype(F32) + zlo_swap(pair).astype(F32)
        act, d_hidden = activate(pair[0], pair[1])
        d_hidden = double(d_hidden, y_swap, (1, 3))
        act = double(act, y_swap, (3, 1))
        grad_in = lax.dot_general(a, d_hidden, first_dims, preferred_element_type=F32)
        grad_out = lax.dot_general(act, u, first_dims, preferred_element_type=F32)
        part_x = lax.dot_general(d_hidden, w_in, last_dims, preferred_element_type=F32).astype(BF16)
        return grad_in, grad_out, part_x.reshape(RING, RING, LOW, WIDTH)

    def over_x(parts):
        kept = jnp.stack([p[:2, s] for s in (0, 1) for p in parts])
        sent = jnp.stack([p[:2, s] for s in (2, 3) for p in parts])
        upper = halve(kept, sent, x_swap, (1, 3))
        kept = jnp.stack([p[2:, s] for s in (0, 2) for p in parts])
        sent = jnp.stack([p[2:, s] for s in (1, 3) for p in parts])
        lower = halve(kept, sent, x_swap, (3, 1))
        return [jnp.concatenate([upper[i], lower[i]]).reshape(ROWS, WIDTH) for i in range(len(parts))]

    grads = [chunk(a_own, u_own)] + [chunk(*spread(got)) for got in (got_1, got_3, got_2)]
    grad_x, part_1, part_3 = over_x([g[2] for g in grads[:3]])
    (part_2,) = over_x([grads[3][2]])
    for part, pair in ((part_1, 1), (part_3, 3), (part_2, 2)):
        grad_x = grad_x + zhi_swap(part.astype(BF16), pair).astype(F32)
    at = jnp.arange(ROWS, dtype=jnp.int32)
    place = jnp.array([NEAR.index(k) for k in range(RING)], jnp.int32)[at // LOW ^ y]
    grad_x = row_order(grad_x.astype(BF16), place * LOW + at % LOW)

    grad_in = sum(g[0] for g in grads)
    grad_out = sum(g[1] for g in grads)
    grad_in = grad_in[:, :HALF] + core_swap(grad_in[:, HALF:].astype(BF16)).astype(F32)
    grad_out = grad_out[:HALF] + core_swap(grad_out[HALF:].astype(BF16)).astype(F32)
    return (grad_x, grad_in.astype(BF16), grad_out.astype(BF16))


def solution(mesh):
    return jax.shard_map(
        on_device,
        mesh=mesh,
        in_specs=(P("depth", "row"), P("depth", "row"), P("row", "col"), P("col", "row")),
        out_specs=(
            P(("depth", "col"), "row"),
            P("row", ("col", "depth")),
            P(("col", "depth"), "row"),
        ),
        check_vma=False,
    )
```

```python
import jax
import jax.numpy as jnp
from jax import lax
from jax.sharding import PartitionSpec as P

RING = 4
SLAB = 512
ROWS = 128
LOW = 32
WIDTH = 768
UNITS = 768
HALF = UNITS // 2
BF16 = jnp.bfloat16
F32 = jnp.float32

NEAR = (0, 3, 1, 2)
FAR = (0, 1, 3, 2)

last_dims = (((1,), (1,)), ((), ()))
first_dims = (((0,), (0,)), ((), ()))


def activation(values):
    return jax.nn.gelu(values, approximate=True)


def activate(hidden, d_act):
    act_full, pullback = jax.vjp(activation, hidden)
    return act_full.astype(BF16), pullback(d_act)[0].astype(BF16)


def y_swap(values, pair):
    return lax.ppermute(values, "row", [(r, r ^ pair) for r in range(8)])


def zlo_swap(values):
    return lax.ppermute(values, "row", [(r, r ^ 4) for r in range(8)])


def x_swap(values, pair):
    return lax.ppermute(values, "col", [(c, c ^ pair) for c in range(RING)])


def zhi_swap(values, pair):
    return lax.ppermute(values, "depth", [(d, d ^ (2 * pair)) for d in range(8)])


def core_swap(values):
    return lax.ppermute(values, "depth", [(d, d ^ 1) for d in range(8)])


def halve(kept, sent, swap, pairs):
    both = kept.astype(F32) + swap(sent.astype(BF16), pairs[0]).astype(F32)
    span = both.shape[0] // 2
    return both[:span] + swap(both[span:].astype(BF16), pairs[1]).astype(F32)


def double(own, swap, pairs):
    two = jnp.concatenate([own, swap(own, pairs[1])])
    return jnp.concatenate([two, swap(two, pairs[0])])


def row_order(rows, source):
    pick = source[:, None] == lax.broadcasted_iota(jnp.int32, (source.shape[0], rows.shape[0]), 1)
    return jnp.dot(pick.astype(BF16), rows, preferred_element_type=F32).astype(BF16)


def on_device(inputs, upstream, w_in, w_out):
    depth = lax.axis_index("depth")
    x = lax.axis_index("col")
    zhi, core = depth // 2, depth % 2
    y = lax.axis_index("row") % RING

    ats = [zhi * UNITS + c * HALF for c in (core, 1 - core)]
    w_in = jnp.concatenate([lax.dynamic_slice_in_dim(w_in, at, HALF, 1) for at in ats], 1)
    w_out = jnp.concatenate([lax.dynamic_slice_in_dim(w_out, at, HALF, 0) for at in ats], 0)

    at = jnp.arange(SLAB, dtype=jnp.int32)

    def order(order_y, place):
        order_y, order_x = (jnp.array(o, jnp.int32) for o in (order_y, NEAR))
        return (order_x[place // LOW % RING] ^ x) * ROWS + (order_y[place // ROWS] ^ y) * LOW + place % LOW

    a_own = row_order(inputs, order(NEAR, at))
    u_own = row_order(upstream, order(FAR, at))

    quarter = jnp.stack([v.reshape(RING, RING, LOW, WIDTH)[:, 0] for v in (a_own, u_own)])
    got_1 = zhi_swap(quarter, 1)
    got_3 = zhi_swap(quarter, 3)
    got_2 = (zhi_swap(got_1[0], 3), zhi_swap(got_3[1], 1))

    def behind(values, steps):
        return values + sum(step.reshape(-1, WIDTH)[:1] for step in steps).astype(values.dtype) * 0

    def spread(quarter, steps):
        if steps:
            quarter = [behind(q, steps) for q in quarter]
        one_a = x_swap(quarter[0], 1)
        three_u = x_swap(quarter[1], 3)
        far_a = x_swap(jnp.stack([quarter[0], one_a]), 3)
        far_u = x_swap(jnp.stack([quarter[1], three_u]), 1)
        a = jnp.stack([quarter[0], far_a[0], one_a, far_a[1]], 1)
        u = jnp.stack([quarter[1], three_u, far_u[0], far_u[1]], 1)
        return a.reshape(SLAB, WIDTH), u.reshape(SLAB, WIDTH), (far_a, far_u)

    def chunk(a, u, steps):
        part_hidden = jnp.dot(a, w_in, preferred_element_type=F32)
        part_grad = lax.dot_general(u, w_out, last_dims, preferred_element_type=F32)
        if steps:
            part_hidden, part_grad = behind(part_hidden, steps), behind(part_grad, steps)
        part_hidden, part_grad = part_hidden.astype(BF16), part_grad.astype(BF16)
        hidden = halve(part_hidden[:SLAB // 2], part_hidden[SLAB // 2:], y_swap, (1, 3))
        d_act = halve(part_grad[:SLAB // 2], part_grad[SLAB // 2:], y_swap, (3, 1))
        steps = (hidden, d_act)
        pair = jnp.stack(steps).astype(BF16)
        pair = pair.astype(F32) + zlo_swap(pair).astype(F32)
        act, d_hidden = activate(pair[0], pair[1])
        d_hidden = double(d_hidden, y_swap, (1, 3))
        act = double(act, y_swap, (3, 1))
        grad_in = lax.dot_general(a, d_hidden, first_dims, preferred_element_type=F32)
        grad_out = lax.dot_general(act, u, first_dims, preferred_element_type=F32)
        part_x = lax.dot_general(d_hidden, w_in, last_dims, preferred_element_type=F32).astype(BF16)
        return (grad_in, grad_out, part_x.reshape(RING, RING, LOW, WIDTH)), steps

    def over_x(parts):
        kept = jnp.stack([p[:2, s] for s in (0, 1) for p in parts])
        sent = jnp.stack([p[:2, s] for s in (2, 3) for p in parts])
        upper = halve(kept, sent, x_swap, (1, 3))
        kept = jnp.stack([p[2:, s] for s in (0, 2) for p in parts])
        sent = jnp.stack([p[2:, s] for s in (1, 3) for p in parts])
        lower = halve(kept, sent, x_swap, (3, 1))
        return [jnp.concatenate([upper[i], lower[i]]).reshape(ROWS, WIDTH) for i in range(len(parts))]

    result, summed = chunk(a_own, u_own, ())
    grads, spread_steps = [result], ()
    for got in (got_1, got_2, got_3):
        a, u, spread_steps = spread(got, spread_steps)
        result, summed = chunk(a, u, summed)
        grads.append(result)
    grad_x, part_1, part_2 = over_x([g[2] for g in grads[:3]])
    (part_3,) = over_x([grads[3][2]])
    for part, pair in ((part_1, 1), (part_2, 2), (part_3, 3)):
        grad_x = grad_x + zhi_swap(part.astype(BF16), pair).astype(F32)
    at = jnp.arange(ROWS, dtype=jnp.int32)
    place = jnp.array([NEAR.index(k) for k in range(RING)], jnp.int32)[at // LOW ^ y]
    grad_x = row_order(grad_x.astype(BF16), place * LOW + at % LOW)

    grad_in = sum(g[0] for g in grads)
    grad_out = sum(g[1] for g in grads)
    grad_in = grad_in[:, :HALF] + core_swap(grad_in[:, HALF:].astype(BF16)).astype(F32)
    grad_out = grad_out[:HALF] + core_swap(grad_out[HALF:].astype(BF16)).astype(F32)
    return (grad_x, grad_in.astype(BF16), grad_out.astype(BF16))


def solution(mesh):
    return jax.shard_map(
        on_device,
        mesh=mesh,
        in_specs=(P("depth", "row"), P("depth", "row"), P("row", "col"), P("col", "row")),
        out_specs=(
            P(("depth", "col"), "row"),
            P("row", ("col", "depth")),
            P(("col", "depth"), "row"),
        ),
        check_vma=False,
    )
```

```python
import jax
import jax.numpy as jnp
from jax import lax
from jax.sharding import PartitionSpec as P

RING = 4
SLAB = 512
ROWS = 128
LOW = 32
WIDTH = 768
UNITS = 768
HALF = UNITS // 2
BF16 = jnp.bfloat16
F32 = jnp.float32

NEAR = (0, 3, 1, 2)
FAR = (0, 1, 3, 2)

last_dims = (((1,), (1,)), ((), ()))
first_dims = (((0,), (0,)), ((), ()))


def activation(values):
    return jax.nn.gelu(values, approximate=True)


def activate(hidden, d_act):
    act_full, pullback = jax.vjp(activation, hidden)
    return act_full.astype(BF16), pullback(d_act)[0].astype(BF16)


def y_swap(values, pair):
    return lax.ppermute(values, "row", [(r, r ^ pair) for r in range(8)])


def zlo_swap(values):
    return lax.ppermute(values, "row", [(r, r ^ 4) for r in range(8)])


def x_swap(values, pair):
    return lax.ppermute(values, "col", [(c, c ^ pair) for c in range(RING)])


def zhi_swap(values, pair):
    return lax.ppermute(values, "depth", [(d, d ^ (2 * pair)) for d in range(8)])


def core_swap(values):
    return lax.ppermute(values, "depth", [(d, d ^ 1) for d in range(8)])


def halve(kept, sent, swap, pairs):
    first = swap(sent.astype(BF16), pairs[0])
    both = kept.astype(F32) + first.astype(F32)
    span = both.shape[0] // 2
    return both[:span] + swap(both[span:].astype(BF16), pairs[1]).astype(F32), first


def double(own, swap, pairs):
    two = jnp.concatenate([own, swap(own, pairs[1])])
    return jnp.concatenate([two, swap(two, pairs[0])])


def row_order(rows, source):
    pick = source[:, None] == lax.broadcasted_iota(jnp.int32, (source.shape[0], rows.shape[0]), 1)
    return jnp.dot(pick.astype(BF16), rows, preferred_element_type=F32).astype(BF16)


def on_device(inputs, upstream, w_in, w_out):
    depth = lax.axis_index("depth")
    x = lax.axis_index("col")
    zhi, core = depth // 2, depth % 2
    y = lax.axis_index("row") % RING

    ats = [zhi * UNITS + c * HALF for c in (core, 1 - core)]
    w_in = jnp.concatenate([lax.dynamic_slice_in_dim(w_in, at, HALF, 1) for at in ats], 1)
    w_out = jnp.concatenate([lax.dynamic_slice_in_dim(w_out, at, HALF, 0) for at in ats], 0)

    at = jnp.arange(SLAB, dtype=jnp.int32)

    def order(order_y, place):
        order_y, order_x = (jnp.array(o, jnp.int32) for o in (order_y, NEAR))
        return (order_x[place // LOW % RING] ^ x) * ROWS + (order_y[place // ROWS] ^ y) * LOW + place % LOW

    a_own = row_order(inputs, order(NEAR, at))
    u_own = row_order(upstream, order(FAR, at))

    quarter = jnp.stack([v.reshape(RING, RING, LOW, WIDTH)[:, 0] for v in (a_own, u_own)])
    got_1 = zhi_swap(quarter, 1)
    got_3 = zhi_swap(quarter, 3)

    def behind(values, steps):
        return values + sum(step.reshape(-1, WIDTH)[:1] for step in steps).astype(values.dtype) * 0

    def spread(quarter, steps):
        quarter = [behind(q, steps) if steps else q for q in quarter]
        return quarter, (x_swap(quarter[0], 1), x_swap(quarter[1], 3))

    def spread_whole(quarter, first):
        one_a, three_u = first
        far_a = x_swap(jnp.stack([quarter[0], one_a]), 3)
        far_u = x_swap(jnp.stack([quarter[1], three_u]), 1)
        a = jnp.stack([quarter[0], far_a[0], one_a, far_a[1]], 1)
        u = jnp.stack([quarter[1], three_u, far_u[0], far_u[1]], 1)
        return a.reshape(SLAB, WIDTH), u.reshape(SLAB, WIDTH), (far_a, far_u)

    def chunk(a, u, steps):
        part_hidden = jnp.dot(a, w_in, preferred_element_type=F32)
        part_grad = lax.dot_general(u, w_out, last_dims, preferred_element_type=F32)
        if steps:
            part_hidden, part_grad = behind(part_hidden, steps), behind(part_grad, steps)
        part_hidden, part_grad = part_hidden.astype(BF16), part_grad.astype(BF16)
        hidden, came_hidden = halve(part_hidden[:SLAB // 2], part_hidden[SLAB // 2:], y_swap, (1, 3))
        d_act, came_grad = halve(part_grad[:SLAB // 2], part_grad[SLAB // 2:], y_swap, (3, 1))
        pair = jnp.stack([hidden, d_act]).astype(BF16)
        pair = pair.astype(F32) + zlo_swap(pair).astype(F32)
        act, d_hidden = activate(pair[0], pair[1])
        d_hidden = double(d_hidden, y_swap, (1, 3))
        act = double(act, y_swap, (3, 1))
        grad_in = lax.dot_general(a, d_hidden, first_dims, preferred_element_type=F32)
        grad_out = lax.dot_general(act, u, first_dims, preferred_element_type=F32)
        part_x = lax.dot_general(d_hidden, w_in, last_dims, preferred_element_type=F32).astype(BF16)
        return (grad_in, grad_out, part_x.reshape(RING, RING, LOW, WIDTH)), (came_hidden, came_grad)

    def over_x(parts):
        kept = jnp.stack([p[:2, s] for s in (0, 1) for p in parts])
        sent = jnp.stack([p[:2, s] for s in (2, 3) for p in parts])
        upper, _ = halve(kept, sent, x_swap, (1, 3))
        kept = jnp.stack([p[2:, s] for s in (0, 2) for p in parts])
        sent = jnp.stack([p[2:, s] for s in (1, 3) for p in parts])
        lower, _ = halve(kept, sent, x_swap, (3, 1))
        return [jnp.concatenate([upper[i], lower[i]]).reshape(ROWS, WIDTH) for i in range(len(parts))]

    result, came = chunk(a_own, u_own, ())
    grads = [result]
    quarter, first = spread(got_1, ())
    got_2 = (zhi_swap(behind(got_1[0], first), 3), zhi_swap(behind(got_3[1], first), 1))
    for after in (got_2, got_3, None):
        a, u, steps = spread_whole(quarter, first)
        if after is not None:
            quarter, first = spread(after, steps)
        result, came = chunk(a, u, came)
        grads.append(result)

    grad_x, part_1 = over_x([g[2] for g in grads[:2]])
    came_1 = zhi_swap(part_1.astype(BF16), 1)
    (part_2,) = over_x([grads[2][2]])
    (part_3,) = over_x([behind(grads[3][2], (came_1,))])
    came_2 = zhi_swap(part_2.astype(BF16), 2)
    came_3 = zhi_swap(part_3.astype(BF16), 3)
    grad_x = grad_x + came_1.astype(F32) + came_2.astype(F32) + came_3.astype(F32)
    grad_in = sum(g[0] for g in grads)
    grad_out = sum(g[1] for g in grads)
    grad_in = grad_in[:, :HALF] + core_swap(grad_in[:, HALF:].astype(BF16)).astype(F32)
    grad_out = grad_out[:HALF] + core_swap(grad_out[HALF:].astype(BF16)).astype(F32)
    grad_in, grad_out = grad_in.astype(BF16), grad_out.astype(BF16)
    grad_x = behind(grad_x, (grad_in[:2], grad_out[:1]))

    at = jnp.arange(ROWS, dtype=jnp.int32)
    place = jnp.array([NEAR.index(k) for k in range(RING)], jnp.int32)[at // LOW ^ y]
    grad_x = row_order(grad_x.astype(BF16), place * LOW + at % LOW)
    return (grad_x, grad_in, grad_out)


def solution(mesh):
    return jax.shard_map(
        on_device,
        mesh=mesh,
        in_specs=(P("depth", "row"), P("depth", "row"), P("row", "col"), P("col", "row")),
        out_specs=(
            P(("depth", "col"), "row"),
            P("row", ("col", "depth")),
            P(("col", "depth"), "row"),
        ),
        check_vma=False,
    )
```

```python
import jax
import jax.numpy as jnp
from jax import lax
from jax.sharding import PartitionSpec as P

RING = 4
SLAB = 512
ROWS = 128
LOW = 32
WIDTH = 768
UNITS = 768
HALF = UNITS // 2
BF16 = jnp.bfloat16
F32 = jnp.float32

NEAR = (0, 3, 1, 2)
FAR = (0, 1, 3, 2)

last_dims = (((1,), (1,)), ((), ()))
first_dims = (((0,), (0,)), ((), ()))


def activation(values):
    return jax.nn.gelu(values, approximate=True)


def activate(hidden, d_act):
    act_full, pullback = jax.vjp(activation, hidden)
    return act_full.astype(BF16), pullback(d_act)[0].astype(BF16)


def y_swap(values, pair):
    return lax.ppermute(values, "row", [(r, r ^ pair) for r in range(8)])


def zlo_swap(values):
    return lax.ppermute(values, "row", [(r, r ^ 4) for r in range(8)])


def x_swap(values, pair):
    return lax.ppermute(values, "col", [(c, c ^ pair) for c in range(RING)])


def zhi_swap(values, pair):
    return lax.ppermute(values, "depth", [(d, d ^ (2 * pair)) for d in range(8)])


def core_swap(values):
    return lax.ppermute(values, "depth", [(d, d ^ 1) for d in range(8)])


def halve(kept, sent, swap, pairs):
    first = swap(sent.astype(BF16), pairs[0])
    both = kept.astype(F32) + first.astype(F32)
    span = both.shape[0] // 2
    return both[:span] + swap(both[span:].astype(BF16), pairs[1]).astype(F32), first


def double(own, swap, pairs):
    two = jnp.concatenate([own, swap(own, pairs[1])])
    return jnp.concatenate([two, swap(two, pairs[0])])


def row_order(rows, source):
    pick = source[:, None] == lax.broadcasted_iota(jnp.int32, (source.shape[0], rows.shape[0]), 1)
    return jnp.dot(pick.astype(BF16), rows, preferred_element_type=F32).astype(BF16)


def on_device(inputs, upstream, w_in, w_out):
    depth = lax.axis_index("depth")
    x = lax.axis_index("col")
    zhi, core = depth // 2, depth % 2
    y = lax.axis_index("row") % RING

    ats = [zhi * UNITS + c * HALF for c in (core, 1 - core)]
    w_in = jnp.concatenate([lax.dynamic_slice_in_dim(w_in, at, HALF, 1) for at in ats], 1)
    w_out = jnp.concatenate([lax.dynamic_slice_in_dim(w_out, at, HALF, 0) for at in ats], 0)

    at = jnp.arange(SLAB, dtype=jnp.int32)

    def order(order_y, place):
        order_y, order_x = (jnp.array(o, jnp.int32) for o in (order_y, NEAR))
        return (order_x[place // LOW % RING] ^ x) * ROWS + (order_y[place // ROWS] ^ y) * LOW + place % LOW

    a_own = row_order(inputs, order(NEAR, at))
    u_own = row_order(upstream, order(FAR, at))

    quarter = jnp.stack([v.reshape(RING, RING, LOW, WIDTH)[:, 0] for v in (a_own, u_own)])
    got_1 = zhi_swap(quarter, 1)
    got_3 = zhi_swap(quarter, 3)

    def behind(values, steps):
        return values + sum(step.reshape(-1, WIDTH)[:1] for step in steps).astype(values.dtype) * 0

    def spread(quarter, steps):
        quarter = [behind(q, steps) if steps else q for q in quarter]
        return quarter, (x_swap(quarter[0], 1), x_swap(quarter[1], 3))

    def spread_whole(quarter, first):
        one_a, three_u = first
        far_a = x_swap(jnp.stack([quarter[0], one_a]), 3)
        far_u = x_swap(jnp.stack([quarter[1], three_u]), 1)
        parts_a, parts_u = (quarter[0], far_a[0], one_a, far_a[1]), (quarter[1], three_u, far_u[0], far_u[1])
        slabs = range(one_a.shape[0])
        a, u = (
            jnp.stack([part[i] for i in slabs for part in parts], 1).reshape(-1, WIDTH) for parts in (parts_a, parts_u)
        )
        return a, u, (far_a, far_u)

    def chunk(a, u, steps):
        part_hidden = jnp.dot(a, w_in, preferred_element_type=F32)
        part_grad = lax.dot_general(u, w_out, last_dims, preferred_element_type=F32)
        if steps:
            part_hidden, part_grad = behind(part_hidden, steps), behind(part_grad, steps)
        part_hidden, part_grad = part_hidden.astype(BF16), part_grad.astype(BF16)
        span = a.shape[0] // 2
        hidden, came_hidden = halve(part_hidden[:span], part_hidden[span:], y_swap, (1, 3))
        d_act, came_grad = halve(part_grad[:span], part_grad[span:], y_swap, (3, 1))
        pair = jnp.stack([hidden, d_act]).astype(BF16)
        pair = pair.astype(F32) + zlo_swap(pair).astype(F32)
        act, d_hidden = activate(pair[0], pair[1])
        d_hidden = double(d_hidden, y_swap, (1, 3))
        act = double(act, y_swap, (3, 1))
        grad_in = lax.dot_general(a, d_hidden, first_dims, preferred_element_type=F32)
        grad_out = lax.dot_general(act, u, first_dims, preferred_element_type=F32)
        part_x = lax.dot_general(d_hidden, w_in, last_dims, preferred_element_type=F32).astype(BF16)
        part_x = part_x.reshape(RING, -1, RING, LOW, WIDTH)
        return (grad_in, grad_out, [part_x[:, i] for i in range(part_x.shape[1])]), (came_hidden, came_grad)

    def over_x(parts):
        kept = jnp.stack([p[:2, s] for s in (0, 1) for p in parts])
        sent = jnp.stack([p[:2, s] for s in (2, 3) for p in parts])
        upper, _ = halve(kept, sent, x_swap, (1, 3))
        kept = jnp.stack([p[2:, s] for s in (0, 2) for p in parts])
        sent = jnp.stack([p[2:, s] for s in (1, 3) for p in parts])
        lower, _ = halve(kept, sent, x_swap, (3, 1))
        return [jnp.concatenate([upper[i], lower[i]]).reshape(ROWS, WIDTH) for i in range(len(parts))]

    result, came = chunk(a_own, u_own, ())
    grads = [result]
    quarter, first = spread([jnp.stack([got_1[i], got_3[i]]) for i in range(2)], ())
    got_2 = (zhi_swap(behind(got_1[0], first), 3), zhi_swap(behind(got_3[1], first), 1))
    a, u, steps = spread_whole(quarter, first)
    quarter, first = spread([got[None] for got in got_2], steps)
    result, came = chunk(a, u, came)
    grads.append(result)
    a, u, _ = spread_whole(quarter, first)
    result, came = chunk(a, u, came)
    grads.append(result)

    grad_x, part_2 = over_x(grads[0][2] + grads[2][2])
    part_1, part_3 = over_x(grads[1][2])
    for part, pair in ((part_2, 2), (part_1, 1), (part_3, 3)):
        grad_x = grad_x + zhi_swap(part.astype(BF16), pair).astype(F32)
    grad_in = sum(g[0] for g in grads)
    grad_out = sum(g[1] for g in grads)
    grad_in = grad_in[:, :HALF] + core_swap(grad_in[:, HALF:].astype(BF16)).astype(F32)
    grad_out = grad_out[:HALF] + core_swap(grad_out[HALF:].astype(BF16)).astype(F32)
    grad_in, grad_out = grad_in.astype(BF16), grad_out.astype(BF16)
    grad_x = behind(grad_x, (grad_in[:2], grad_out[:1]))

    at = jnp.arange(ROWS, dtype=jnp.int32)
    place = jnp.array([NEAR.index(k) for k in range(RING)], jnp.int32)[at // LOW ^ y]
    grad_x = row_order(grad_x.astype(BF16), place * LOW + at % LOW)
    return (grad_x, grad_in, grad_out)


def solution(mesh):
    return jax.shard_map(
        on_device,
        mesh=mesh,
        in_specs=(P("depth", "row"), P("depth", "row"), P("row", "col"), P("col", "row")),
        out_specs=(
            P(("depth", "col"), "row"),
            P("row", ("col", "depth")),
            P(("col", "depth"), "row"),
        ),
        check_vma=False,
    )
```

```python
import jax
import jax.numpy as jnp
from jax import lax
from jax.sharding import PartitionSpec as P

RING = 4
SLAB = 512
ROWS = 128
LOW = 32
WIDTH = 768
UNITS = 768
HALF = UNITS // 2
BF16 = jnp.bfloat16
F32 = jnp.float32

NEAR = (0, 3, 1, 2)
FAR = (0, 1, 3, 2)

last_dims = (((1,), (1,)), ((), ()))
first_dims = (((0,), (0,)), ((), ()))


def activation(values):
    return jax.nn.gelu(values, approximate=True)


def activate(hidden, d_act):
    act_full, pullback = jax.vjp(activation, hidden)
    return act_full.astype(BF16), pullback(d_act)[0].astype(BF16)


def y_swap(values, pair):
    return lax.ppermute(values, "row", [(r, r ^ pair) for r in range(8)])


def zlo_swap(values):
    return lax.ppermute(values, "row", [(r, r ^ 4) for r in range(8)])


def x_swap(values, pair):
    return lax.ppermute(values, "col", [(c, c ^ pair) for c in range(RING)])


def zhi_swap(values, pair):
    return lax.ppermute(values, "depth", [(d, d ^ (2 * pair)) for d in range(8)])


def core_swap(values):
    return lax.ppermute(values, "depth", [(d, d ^ 1) for d in range(8)])


def halve(kept, sent, swap, pairs):
    first = swap(sent.astype(BF16), pairs[0])
    both = kept.astype(F32) + first.astype(F32)
    span = both.shape[0] // 2
    return both[:span] + swap(both[span:].astype(BF16), pairs[1]).astype(F32), first


def double(own, swap, pairs):
    two = jnp.concatenate([own, swap(own, pairs[1])])
    return jnp.concatenate([two, swap(two, pairs[0])])


def row_order(rows, source):
    pick = source[:, None] == lax.broadcasted_iota(jnp.int32, (source.shape[0], rows.shape[0]), 1)
    return jnp.dot(pick.astype(BF16), rows, preferred_element_type=F32).astype(BF16)


def on_device(inputs, upstream, w_in, w_out):
    depth = lax.axis_index("depth")
    x = lax.axis_index("col")
    zhi, core = depth // 2, depth % 2
    y = lax.axis_index("row") % RING

    ats = [zhi * UNITS + c * HALF for c in (core, 1 - core)]
    w_in = jnp.concatenate([lax.dynamic_slice_in_dim(w_in, at, HALF, 1) for at in ats], 1)
    w_out = jnp.concatenate([lax.dynamic_slice_in_dim(w_out, at, HALF, 0) for at in ats], 0)

    at = jnp.arange(SLAB, dtype=jnp.int32)

    def order(order_y, place):
        order_y, order_x = (jnp.array(o, jnp.int32) for o in (order_y, NEAR))
        return (order_x[place // LOW % RING] ^ x) * ROWS + (order_y[place // ROWS] ^ y) * LOW + place % LOW

    a_own = row_order(inputs, order(NEAR, at))
    u_own = row_order(upstream, order(FAR, at))

    quarter = jnp.stack([v.reshape(RING, RING, LOW, WIDTH)[:, 0] for v in (a_own, u_own)])
    got_1 = zhi_swap(quarter, 1)
    got_3 = zhi_swap(quarter, 3)

    def behind(values, steps):
        return values + sum(step.reshape(-1, WIDTH)[:1] for step in steps).astype(values.dtype) * 0

    def spread(quarter, steps):
        quarter = [behind(q, steps) if steps else q for q in quarter]
        return quarter, (x_swap(quarter[0], 1), x_swap(quarter[1], 3))

    def spread_whole(quarter, first):
        one_a, three_u = first
        far_a = x_swap(jnp.stack([quarter[0], one_a]), 3)
        far_u = x_swap(jnp.stack([quarter[1], three_u]), 1)
        parts_a, parts_u = (quarter[0], far_a[0], one_a, far_a[1]), (quarter[1], three_u, far_u[0], far_u[1])
        slabs = range(one_a.shape[0])
        a, u = (
            jnp.stack([part[i] for i in slabs for part in parts], 1).reshape(-1, WIDTH) for parts in (parts_a, parts_u)
        )
        return a, u, (far_a, far_u)

    def chunk(a, u, steps):
        part_hidden = jnp.dot(a, w_in, preferred_element_type=F32)
        part_grad = lax.dot_general(u, w_out, last_dims, preferred_element_type=F32)
        if steps:
            part_hidden, part_grad = behind(part_hidden, steps), behind(part_grad, steps)
        part_hidden, part_grad = part_hidden.astype(BF16), part_grad.astype(BF16)
        span = a.shape[0] // 2
        hidden, _ = halve(part_hidden[:span], part_hidden[span:], y_swap, (1, 3))
        d_act, _ = halve(part_grad[:span], part_grad[span:], y_swap, (3, 1))
        pair = jnp.stack([hidden, d_act]).astype(BF16)
        pair = pair.astype(F32) + zlo_swap(pair).astype(F32)
        act, d_hidden = activate(pair[0], pair[1])
        d_hidden = double(d_hidden, y_swap, (1, 3))
        act = double(act, y_swap, (3, 1))
        grad_in = lax.dot_general(a, d_hidden, first_dims, preferred_element_type=F32)
        grad_out = lax.dot_general(act, u, first_dims, preferred_element_type=F32)
        part_x = lax.dot_general(d_hidden, w_in, last_dims, preferred_element_type=F32).astype(BF16)
        part_x = part_x.reshape(RING, -1, RING, LOW, WIDTH)
        return (grad_in, grad_out, [part_x[:, i] for i in range(part_x.shape[1])]), (hidden, d_act)

    def over_x(parts):
        kept = jnp.stack([p[:2, s] for s in (0, 1) for p in parts])
        sent = jnp.stack([p[:2, s] for s in (2, 3) for p in parts])
        upper, _ = halve(kept, sent, x_swap, (1, 3))
        kept = jnp.stack([p[2:, s] for s in (0, 2) for p in parts])
        sent = jnp.stack([p[2:, s] for s in (1, 3) for p in parts])
        lower, _ = halve(kept, sent, x_swap, (3, 1))
        return [jnp.concatenate([upper[i], lower[i]]).reshape(ROWS, WIDTH) for i in range(len(parts))]

    result, came = chunk(a_own, u_own, ())
    grads = [result]
    quarter, first = spread([jnp.stack([got_1[i], got_3[i]]) for i in range(2)], ())
    got_2 = (zhi_swap(behind(got_1[0], first), 3), zhi_swap(behind(got_3[1], first), 1))
    a, u, steps = spread_whole(quarter, first)
    quarter, first = spread([got[None] for got in got_2], steps)
    result, came = chunk(a, u, came)
    grads.append(result)
    a, u, _ = spread_whole(quarter, first)
    result, came = chunk(a, u, came)
    grads.append(result)

    grad_x, part_2 = over_x(grads[0][2] + grads[2][2])
    part_1, part_3 = over_x(grads[1][2])
    for part, pair in ((part_2, 2), (part_1, 1), (part_3, 3)):
        grad_x = grad_x + zhi_swap(part.astype(BF16), pair).astype(F32)
    grad_in = sum(g[0] for g in grads)
    grad_out = sum(g[1] for g in grads)
    grad_in = grad_in[:, :HALF] + core_swap(grad_in[:, HALF:].astype(BF16)).astype(F32)
    grad_out = grad_out[:HALF] + core_swap(grad_out[HALF:].astype(BF16)).astype(F32)
    grad_in, grad_out = grad_in.astype(BF16), grad_out.astype(BF16)
    grad_x = behind(grad_x, (grad_in[:2], grad_out[:1]))

    at = jnp.arange(ROWS, dtype=jnp.int32)
    place = jnp.array([NEAR.index(k) for k in range(RING)], jnp.int32)[at // LOW ^ y]
    grad_x = row_order(grad_x.astype(BF16), place * LOW + at % LOW)
    return (grad_x, grad_in, grad_out)


def solution(mesh):
    return jax.shard_map(
        on_device,
        mesh=mesh,
        in_specs=(P("depth", "row"), P("depth", "row"), P("row", "col"), P("col", "row")),
        out_specs=(
            P(("depth", "col"), "row"),
            P("row", ("col", "depth")),
            P(("col", "depth"), "row"),
        ),
        check_vma=False,
    )
```
